256 devices in a mesh: dp: 4 (over z_lo, core), seq: 64 (over z_hi, y, x).
Axes of the slice: x: 4, y: 4, z: 8 (z_hi: 4, z_lo: 2; z = z_hi * 2 + z_lo), core: 2. Of those that a mesh axis runs over, the one named last changes fastest.
Arguments:
- glu_out: bfloat16 [4, 8192, 1536], P('dp', 'seq'), may hold values from -6 to 6
- lengths: int32 [4], replicated, may hold values from 1024 to 8192, as said below
- kernel: float32 [31, 1536], replicated, may hold values from -1 to 1
- gain: float32 [1536], replicated, may hold values from 0.25 to 1.75
- bias: float32 [1536], replicated, may hold values from -3 to 3
- weight: bfloat16 [1536, 1536], P(('dp', 'seq')), may hold values from -0.15625 to 0.15625
- master: float32 [1536, 1536], P(('dp', 'seq')), may hold values from -0.15625 to 0.15625
- moment_one: float32 [1536, 1536], P(('dp', 'seq')), may hold values from -120 to 120
- moment_two: float32 [1536, 1536], P(('dp', 'seq')), may hold values from 100 to 100000
- cotangent: bfloat16 [4, 8192, 1536], P('dp', 'seq'), may hold values from -6 to 6
Outputs:
- module_out: bfloat16 [4, 8192, 1536], P('dp', 'seq')
- input_grad: bfloat16 [4, 8192, 1536], P('dp', 'seq')
- kernel_grad: float32 [31, 1536], replicated
- gain_grad: float32 [1536], replicated
- bias_grad: float32 [1536], replicated
- new_master: float32 [1536, 1536], P(('dp', 'seq'))
- new_one: float32 [1536, 1536], P(('dp', 'seq'))
- new_two: float32 [1536, 1536], P(('dp', 'seq'))
The draws below stay inside these ranges and needn't reach their ends.
Inputs may be any that keep to these rules, and one draw needn't show every extreme that they name: `lengths`: in every draw one stream has all 8192 frames valid; each other stream has between 1024 and 2730 valid frames.
All inputs are finite; a program needn't handle non-finite values.
Results may differ from the reference program's by a relative error of at most 0.0049.
Values may be sent and summed in bfloat16 or wider, within the bound.
No kernel may reach another device: no remote copies, remote signals or barrier semaphores. Data moves between devices by JAX's collectives and lax.ppermute only.
A program may use at most 64 MiB of HBM per device.

```python
import math
import jax
import jax.numpy as jnp
from jax import lax

D = 1536
KERNEL = 31
HALF = 15
LENGTH = 8192
STREAMS = 4


def draw_lengths(key, part):
    first_key = jax.random.fold_in(key, 11)
    second_key = jax.random.fold_in(key, 23)
    shorter = jax.random.randint(first_key, (STREAMS,), LENGTH // 8, LENGTH // 3 + 1)
    longest = jax.random.randint(second_key, (), 0, STREAMS)
    return jnp.where(jnp.arange(STREAMS) == longest, LENGTH, shorter).astype(jnp.int32)


def block_scale(own_key, extent, cuts, smallest, high):
    level, own = 1.0, jax.random.fold_in(own_key, 6)
    for position, shards_of in cuts:
        draws = jnp.exp(jax.random.uniform(jax.random.fold_in(own, position), (shards_of,), jnp.float32, smallest / len(cuts), high / len(cuts)))
        level = level * jnp.repeat(draws, extent[position] // shards_of).reshape([-1 if axis == position else 1 for axis in range(len(extent))])
    return level


def bell_draw(own_key, shape, scale, reach, shards=(), held_as=jnp.bfloat16):
    result = scale * jax.random.normal(own_key, shape, jnp.float32)
    if shards:
        result = result * block_scale(own_key, shape, shards, -0.22, 0.18)
    return jnp.clip(result, -reach, reach).astype(held_as)


def setup_inputs(seed: int = 0) -> dict:
    key_list = jax.random.split(jax.random.key(seed), 11)
    glu_out = bell_draw(key_list[0], (STREAMS, LENGTH, D), 1.0, 6.0, ((0, 4), (1, 64)))
    lengths = draw_lengths(jax.random.fold_in(key_list[10], 71), 0)
    kernel = bell_draw(key_list[2], (KERNEL, D), KERNEL ** -0.5, 1.0, (), jnp.float32)
    gain = jnp.clip(1.0 + 0.15 * jax.random.normal(key_list[3], (D,), jnp.float32), 0.25, 1.75)
    bias = bell_draw(key_list[4], (D,), 0.5, 3.0, (), jnp.float32)
    weight = bell_draw(key_list[5], (D, D), D ** -0.5, 0.15625, ((0, 256),))
    master = bell_draw(key_list[6], (D, D), D ** -0.5, 0.15625, ((0, 256),), jnp.float32)
    moment_one = bell_draw(key_list[7], (D, D), 20.0, 120.0, ((0, 256),), jnp.float32)
    moment_two = jnp.clip(jnp.exp(math.log(100000.0) - 6.9077553 * jax.random.uniform(key_list[8], (D, D), jnp.float32) ** block_scale(key_list[8], (D, D), ((0, 256),), -0.2, 0.2)), 100.0, 100000.0)
    cotangent = bell_draw(key_list[9], (STREAMS, LENGTH, D), 1.0, 6.0, ((0, 4), (1, 64)))
    return {"glu_out": glu_out, "lengths": lengths, "kernel": kernel, "gain": gain, "bias": bias, "weight": weight, "master": master, "moment_one": moment_one, "moment_two": moment_two, "cotangent": cotangent}


beta_one = 0.9
beta_two = 0.999
adam_rate = 0.001
adam_eps = 1e-08
norm_eps = 1e-05
first_fix = 0.9999734386011124
second_fix = 0.09520785288629043

def taps_apply(padded, kernel, width):
    total = jnp.zeros((width, padded.shape[1]), jnp.float32)
    for tap in range(KERNEL):
        total = total + kernel[tap] * padded[tap:tap + width]
    return total

def prepare(glu_out, lengths, kernel, stream):
    positions = jnp.arange(LENGTH, dtype=jnp.int32)
    valid = (positions < lengths[stream])[:, None]
    masked = jnp.where(valid, glu_out[stream], jnp.zeros((), glu_out.dtype))
    padded = jnp.pad(masked.astype(jnp.float32), ((HALF, HALF), (0, 0)))
    conv_out = taps_apply(padded, kernel, LENGTH)
    return (valid, padded, conv_out)

def backward_part(glu_out, lengths, kernel, gain, bias, weight, cotangent, stream, channel_mean, inv_std):
    valid, padded, conv_out = prepare(glu_out, lengths, kernel, stream)
    standard = (conv_out - channel_mean) * inv_std
    scaled = gain * standard + bias
    logistic = jax.nn.sigmoid(scaled)
    hidden = (scaled * logistic).astype(jnp.bfloat16)
    grad_out = jnp.where(valid, cotangent[stream], jnp.zeros((), cotangent.dtype))
    hidden_grad = lax.dot_general(grad_out, weight, (((1,), (1,)), ((), ())), preferred_element_type=jnp.float32)
    scaled_grad = hidden_grad * logistic * (1.0 + scaled * (1.0 - logistic))
    return (valid, padded, standard, hidden, grad_out, scaled_grad)

def reference(glu_out, lengths, kernel, gain, bias, weight, master, moment_one, moment_two, cotangent):
    count = jnp.sum(lengths).astype(jnp.float32)
    total = jnp.zeros((D,), jnp.float32)
    for stream in range(STREAMS):
        valid, padded, conv_out = prepare(glu_out, lengths, kernel, stream)
        total = total + lax.optimization_barrier(jnp.sum(jnp.where(valid, conv_out, 0.0), axis=0))
    channel_mean = total / count
    spread = jnp.zeros((D,), jnp.float32)
    for stream in range(STREAMS):
        valid, padded, conv_out = prepare(glu_out, lengths, kernel, stream)
        spread = spread + lax.optimization_barrier(jnp.sum(jnp.where(valid, (conv_out - channel_mean) ** 2, 0.0), axis=0))
    inv_std = lax.rsqrt(spread / count + norm_eps)
    outputs = []
    weight_grad = jnp.zeros((D, D), jnp.float32)
    gain_grad = jnp.zeros((D,), jnp.float32)
    bias_grad = jnp.zeros((D,), jnp.float32)
    for stream in range(STREAMS):
        valid, padded, standard, hidden, grad_out, scaled_grad = backward_part(glu_out, lengths, kernel, gain, bias, weight, cotangent, stream, channel_mean, inv_std)
        product = jnp.dot(hidden, weight, preferred_element_type=jnp.float32)
        outputs.append(jnp.where(valid, product, 0.0).astype(jnp.bfloat16))
        weight_grad = weight_grad + lax.dot_general(hidden, grad_out, (((0,), (0,)), ((), ())), preferred_element_type=jnp.float32)
        gain_grad = gain_grad + lax.optimization_barrier(jnp.sum(scaled_grad * standard, axis=0))
        bias_grad = bias_grad + lax.optimization_barrier(jnp.sum(scaled_grad, axis=0))
    grads_in = []
    kernel_grad = jnp.zeros((KERNEL, D), jnp.float32)
    for stream in range(STREAMS):
        valid, padded, standard, hidden, grad_out, scaled_grad = backward_part(glu_out, lengths, kernel, gain, bias, weight, cotangent, stream, channel_mean, inv_std)
        conv_grad = jnp.where(valid, inv_std * (gain * scaled_grad - gain * bias_grad / count - standard * gain * gain_grad / count), 0.0)
        rows_grad = []
        for tap in range(KERNEL):
            rows_grad.append(lax.optimization_barrier(jnp.sum(conv_grad * padded[tap:tap + LENGTH], axis=0)))
        kernel_grad = kernel_grad + jnp.stack(rows_grad)
        grad_pad = jnp.pad(conv_grad, ((HALF, HALF), (0, 0)))
        flipped = jnp.zeros((LENGTH, D), jnp.float32)
        for tap in range(KERNEL):
            flipped = flipped + kernel[tap] * grad_pad[2 * HALF - tap:2 * HALF - tap + LENGTH]
        grads_in.append(jnp.where(valid, flipped, 0.0).astype(jnp.bfloat16))
    new_one = beta_one * moment_one + (1.0 - beta_one) * weight_grad
    new_two = beta_two * moment_two + (1.0 - beta_two) * weight_grad * weight_grad
    new_master = master - adam_rate * (new_one / first_fix) / (jnp.sqrt(new_two / second_fix) + adam_eps)
    return (jnp.stack(outputs), jnp.stack(grads_in), kernel_grad, gain_grad, bias_grad, new_master, new_one, new_two)
```

```python
import jax
import jax.numpy as jnp
from jax import lax
from jax.sharding import Mesh, PartitionSpec as P

KERNEL = 31
HALF = 15
HALO = 32
EDGE = 16

beta_one = 0.9
beta_two = 0.999
adam_rate = 0.001
adam_eps = 1e-08
norm_eps = 1e-05
first_fix = 0.9999734386011124
second_fix = 0.09520785288629043

SEQ = ("zh", "y", "x")
DP = ("zl", "core")
f32 = jnp.float32
bf16 = jnp.bfloat16


def size(axis):
    return lax.axis_size(axis)


def swap(value, axis, mask):
    return lax.ppermute(value, axis, [(i, i ^ mask) for i in range(size(axis))])


def shift(value, axis, step):
    count = size(axis)
    return lax.ppermute(value, axis, [(i, (i + step) % count) for i in range(count)])


def in_order(index, parts):
    odd, high = (index & 1) == 1, (index & 2) == 2
    r0, r1, r2, r3 = parts
    a, b = jnp.where(odd, r1, r0), jnp.where(odd, r0, r1)
    c, d = jnp.where(odd, r3, r2), jnp.where(odd, r2, r3)
    return (jnp.where(high, c, a), jnp.where(high, d, b), jnp.where(high, a, c), jnp.where(high, b, d))


def exchange(value, axis):
    return [value] + [swap(value, axis, m) for m in (1, 2, 3)]


def all_sum(value):
    for axis in ("x", "y", "zh"):
        r = exchange(value, axis)
        value = (r[0] + r[1]) + (r[2] + r[3])
    return value


def gather_rows(weight):
    rows, width = weight.shape
    x = jnp.concatenate(in_order(lax.axis_index("x"), exchange(weight, "x")), axis=0)
    z = jnp.stack(in_order(lax.axis_index("zh"), exchange(x, "zh")), axis=0)
    y = jnp.stack(in_order(lax.axis_index("y"), exchange(z, "y")), axis=1)
    return y.reshape(64 * rows, width)


def scatter_rows(total):
    rows, width = total.shape
    value = total.reshape(4, 4, rows // 16, width)
    for axis, dim in (("y", 1), ("zh", 0), ("x", 0)):
        if axis == "x":
            value = value.reshape(4, rows // 64, width)
        me = lax.axis_index(axis)
        pick = lambda m: lax.dynamic_index_in_dim(value, me ^ m, dim, keepdims=False)
        parts = [pick(0)] + [swap(pick(m).astype(bf16), axis, m).astype(f32) for m in (1, 2, 3)]
        value = (parts[0] + parts[1]) + (parts[2] + parts[3])
    return value


def combine(n, mean, spread):
    for axis in ("x", "y", "zh"):
        r = exchange(jnp.stack([n, mean, spread]), axis)
        counts, means = [p[0] for p in r], [p[1] for p in r]
        n = (counts[0] + counts[1]) + (counts[2] + counts[3])
        some = jnp.maximum(n, 1.0)
        mean = ((counts[0] * means[0] + counts[1] * means[1]) + (counts[2] * means[2] + counts[3] * means[3])) / some
        spread = (r[0][2] + r[1][2]) + (r[2][2] + r[3][2])
        for c, m in zip(counts, means):
            spread = spread + c * (m - mean) * (m - mean)
    return mean, spread


def on_device(
    glu_out, lengths, kernel, gain, bias, weight, master, moment_one, moment_two, cotangent
):
    frames, width = glu_out.shape[1:]
    dp = lax.axis_index(DP)
    seq = lax.axis_index(SEQ)
    own = width // 4
    streams = [dp ^ m for m in range(4)]
    count = jnp.sum(lengths).astype(f32)
    limit = jnp.stack([lengths[s] for s in streams])

    def valid_rows(extra):
        positions = seq * frames - extra + jnp.arange(frames + 2 * extra, dtype=jnp.int32)
        return ((positions >= 0) & (positions < limit[:, None]))[:, :, None]

    def mine(table):
        return lax.dynamic_slice_in_dim(table, dp * own, own, axis=table.ndim - 1)

    taps, gain_own, bias_own = mine(kernel), mine(gain), mine(bias)

    low = shift(glu_out[0, frames - HALO :], SEQ, 1)
    high = shift(glu_out[0, :HALO], SEQ, -1)
    slab = jnp.concatenate([low, glu_out[0], high], axis=0)
    pick = lambda m: lax.dynamic_slice_in_dim(slab, (dp ^ m) * own, own, axis=1)
    slabs = jnp.stack([pick(0)] + [swap(pick(m), DP, m) for m in (1, 2, 3)])
    masked = jnp.where(valid_rows(HALO), slabs, jnp.zeros((), bf16)).astype(f32)

    low = shift(cotangent[0, frames - EDGE :], SEQ, 1)
    high = shift(cotangent[0, :EDGE], SEQ, -1)
    cot = jnp.concatenate([low, cotangent[0], high], axis=0)
    cot_z = swap(cot, "zl", 1)
    pair = swap(jnp.stack([cot, cot_z]), "core", 1)
    grad_out = jnp.stack([cot, pair[0], cot_z, pair[1]])
    grad_out = jnp.where(valid_rows(EDGE), grad_out, jnp.zeros((), bf16))

    rows = gather_rows(weight)

    span = frames + 2 * EDGE
    conv_out = jnp.zeros((4, span, own), f32)
    for tap in range(KERNEL):
        begin = HALO - EDGE - HALF + tap
        conv_out = conv_out + taps[tap] * masked[:, begin : begin + span]

    valid = valid_rows(0)
    inner = conv_out[:, EDGE : EDGE + frames]
    n = jnp.sum(jnp.clip(limit - seq * frames, 0, frames)).astype(f32)
    n = jnp.full((own,), n, f32)
    mean = jnp.sum(jnp.where(valid, inner, 0.0), axis=(0, 1)) / jnp.maximum(n, 1.0)
    off = jnp.where(valid, inner - mean, 0.0)
    channel_mean, spread = combine(n, mean, jnp.sum(off * off, axis=(0, 1)))
    inv_std = lax.rsqrt(spread / count + norm_eps)

    standard = (conv_out - channel_mean) * inv_std
    scaled = gain_own * standard + bias_own
    logistic = jax.nn.sigmoid(scaled)
    hidden = (scaled * logistic)[:, EDGE : EDGE + frames].astype(bf16)
    hidden_grad = lax.dot_general(
        grad_out.reshape(4 * span, width), rows, (((1,), (1,)), ((), ())), preferred_element_type=f32
    ).reshape(4, span, own)
    scaled_grad = hidden_grad * logistic * (1.0 + scaled * (1.0 - logistic))
    inner_grad = scaled_grad[:, EDGE : EDGE + frames]
    sums = all_sum(
        jnp.stack(
            [
                jnp.sum(inner_grad * standard[:, EDGE : EDGE + frames], axis=(0, 1)),
                jnp.sum(inner_grad, axis=(0, 1)),
            ]
        )
    )
    gain_grad, bias_grad = sums[0], sums[1]

    flat = hidden.reshape(4 * frames, own)
    partial = lax.dot_general(
        flat,
        grad_out[:, EDGE : EDGE + frames].reshape(4 * frames, width),
        (((0,), (0,)), ((), ())),
        preferred_element_type=f32,
    )
    weight_grad = scatter_rows(partial)

    product = jnp.dot(flat, rows, preferred_element_type=f32).reshape(4, frames, width)
    other = swap(jnp.stack([product[1], product[3]]).astype(bf16), "core", 1).astype(f32)
    kept, far = product[0] + other[0], product[2] + other[1]
    product = kept + swap(far.astype(bf16), "zl", 1).astype(f32)
    stream_valid = (seq * frames + jnp.arange(frames, dtype=jnp.int32) < limit[0])[:, None]
    module_out = jnp.where(stream_valid, product, 0.0).astype(bf16)

    conv_grad = jnp.where(
        valid_rows(EDGE),
        inv_std
        * (
            gain_own * scaled_grad
            - gain_own * bias_grad / count
            - standard * gain_own * gain_grad / count
        ),
        0.0,
    )
    flipped = jnp.zeros((4, frames, own), f32)
    for tap in range(KERNEL):
        begin = EDGE + HALF - tap
        flipped = flipped + taps[tap] * conv_grad[:, begin : begin + frames]
    flipped = jnp.where(valid, flipped, 0.0).astype(bf16)
    parts = [flipped[0]] + [swap(flipped[m], DP, m) for m in (1, 2, 3)]
    input_grad = jnp.concatenate(in_order(dp, parts), axis=1)

    middle = conv_grad[:, EDGE : EDGE + frames]
    tap_rows = []
    for tap in range(KERNEL):
        begin = HALO - HALF + tap
        tap_rows.append(jnp.sum(middle * masked[:, begin : begin + frames], axis=(0, 1)))
    tap_sums = all_sum(jnp.stack(tap_rows))
    table = jnp.concatenate([tap_sums, sums], axis=0)
    table = jnp.concatenate(in_order(dp, exchange(table, DP)), axis=1)

    new_one = beta_one * moment_one + (1.0 - beta_one) * weight_grad
    new_two = beta_two * moment_two + (1.0 - beta_two) * weight_grad * weight_grad
    new_master = master - adam_rate * (new_one / first_fix) / (
        jnp.sqrt(new_two / second_fix) + adam_eps
    )
    return (
        module_out[None],
        input_grad[None],
        table[:KERNEL],
        table[KERNEL],
        table[KERNEL + 1],
        new_master,
        new_one,
        new_two,
    )


def solution(mesh):
    fine = Mesh(mesh.devices.reshape(2, 2, 4, 4, 4), DP + SEQ)
    whole, split, tall = P(), P(DP, SEQ, None), P(DP + SEQ, None)
    return jax.shard_map(
        on_device,
        mesh=fine,
        in_specs=(split, whole, whole, whole, whole, tall, tall, tall, tall, split),
        out_specs=(split, split, whole, whole, whole, tall, tall, tall),
        check_vma=False,
    )
```

```python
import jax
import jax.numpy as jnp
from jax import lax
from jax.experimental import pallas as pl
from jax.experimental.pallas import tpu as pltpu
from jax.sharding import Mesh, PartitionSpec as P

KERNEL = 31
HALF = 15
HALO = 32
EDGE = 16

beta_one = 0.9
beta_two = 0.999
adam_rate = 0.001
adam_eps = 1e-08
norm_eps = 1e-05
first_fix = 0.9999734386011124
second_fix = 0.09520785288629043

SEQ = ("zh", "y", "x")
DP = ("zl", "core")
f32 = jnp.float32
bf16 = jnp.bfloat16


def size(axis):
    return lax.axis_size(axis)


def swap(value, axis, mask):
    return lax.ppermute(value, axis, [(i, i ^ mask) for i in range(size(axis))])


def shift(value, axis, step):
    count = size(axis)
    return lax.ppermute(value, axis, [(i, (i + step) % count) for i in range(count)])


def in_order(index, parts):
    odd, high = (index & 1) == 1, (index & 2) == 2
    r0, r1, r2, r3 = parts
    a, b = jnp.where(odd, r1, r0), jnp.where(odd, r0, r1)
    c, d = jnp.where(odd, r3, r2), jnp.where(odd, r2, r3)
    return (jnp.where(high, c, a), jnp.where(high, d, b), jnp.where(high, a, c), jnp.where(high, b, d))


def exchange(value, axis):
    return [value] + [swap(value, axis, m) for m in (1, 2, 3)]


barrier = lax.optimization_barrier
STAGES = (("x", 1), ("x", 2), ("zh", 1), ("zh", 2), ("y", 1), ("y", 2))


def halves(value):
    high = lax.reduce_precision(value, 8, 7)
    low = lax.reduce_precision(value - high, 8, 7)
    cut = value.shape[0] // 2
    parts = [high[:cut], high[cut:], low[:cut], low[cut:]]
    return jnp.concatenate(parts, axis=1).astype(bf16)


def whole_again(rows):
    width = rows.shape[1] // 4
    parts = [rows[:, k * width : (k + 1) * width].astype(f32) for k in range(4)]
    return jnp.concatenate([parts[0] + parts[2], parts[1] + parts[3]], axis=0)


def four(parts):
    return (parts[0] + parts[1]) + (parts[2] + parts[3])


def scatter_stage(value, side, axis, dim):
    me = lax.axis_index(axis)
    width = value.shape[-1]
    packed = halves(side)
    blocks = [lax.dynamic_index_in_dim(value, me ^ m, dim, keepdims=False) for m in range(4)]
    kept, sides = [blocks[0]], [whole_again(packed)]
    for m in (1, 2, 3):
        message = jnp.concatenate([blocks[m].astype(bf16).reshape(-1, width), packed], axis=0)
        message = swap(message, axis, m)
        cut = message.shape[0] - packed.shape[0]
        kept.append(message[:cut].astype(f32).reshape(blocks[0].shape))
        sides.append(whole_again(message[cut:]))
    return four(kept), four(sides)


def combine(stats, axis, mask):
    other = swap(stats, axis, mask)
    n = stats[0] + other[0]
    mean = (stats[0] * stats[1] + other[0] * other[1]) / jnp.maximum(n, 1.0)
    here, there = stats[1] - mean, other[1] - mean
    spread = stats[2] + other[2] + stats[0] * here * here + other[0] * there * there
    return jnp.stack([n, mean, spread])


LANES = 128
VMEM_LIMIT = 40 * 1024 * 1024


def valid_in(meta_ref, stream, frames, extra):
    rows = frames + 2 * extra
    place = lax.broadcasted_iota(jnp.int32, (rows, LANES), 0) + (meta_ref[4] * frames - extra)
    return (place >= 0) & (place < meta_ref[stream])


def fold(rows):
    return jnp.sum(rows.reshape(-1, 8, LANES), axis=0)


def squash(rows):
    return jnp.sum(rows, axis=0, keepdims=True)


def conv_kernel(meta_ref, slab_ref, taps_ref, masked_ref, conv_ref, stats_ref):
    span = conv_ref.shape[1]
    frames = span - 2 * EDGE
    half = span // 2
    n = jnp.int32(0)
    total = jnp.zeros((8, LANES), f32)
    for s in range(4):
        n = n + jnp.clip(meta_ref[s] - meta_ref[4] * frames, 0, frames)
        slab = slab_ref[s].astype(f32)
        masked_ref[s] = jnp.where(valid_in(meta_ref, s, frames, HALO), slab, 0.0)
        for part in range(2):
            acc = jnp.zeros((half, LANES), f32)
            for tap in range(KERNEL):
                begin = HALO - EDGE - HALF + tap + part * half
                acc = acc + taps_ref[tap : tap + 1, :] * masked_ref[s, begin : begin + half, :]
            conv_ref[s, part * half : (part + 1) * half, :] = acc
        inner = conv_ref[s, EDGE : EDGE + frames, :]
        total = total + fold(jnp.where(valid_in(meta_ref, s, frames, 0), inner, 0.0))
    number = jnp.full((1, LANES), n, jnp.int32).astype(f32)
    mean = squash(total) / jnp.maximum(number, 1.0)
    spread = jnp.zeros((8, LANES), f32)
    for s in range(4):
        off = conv_ref[s, EDGE : EDGE + frames, :] - mean
        off = jnp.where(valid_in(meta_ref, s, frames, 0), off, 0.0)
        spread = spread + fold(off * off)
    stats_ref[0:1, :] = number
    stats_ref[1:2, :] = mean
    stats_ref[2:3, :] = squash(spread)


def moment_kernel(meta_ref, masked_ref, conv_ref, stats_ref, in_ref, off_ref, ones, offs):
    frames = ones.shape[1]
    for s in range(4):
        valid = valid_in(meta_ref, s, frames, 0)
        ones[s] = jnp.where(valid, 1.0, 0.0)
        offs[s] = jnp.where(valid, conv_ref[s, EDGE : EDGE + frames, :] - stats_ref[1:2, :], 0.0)
    for tap in range(KERNEL):
        begin = HALO - HALF + tap
        plain, centred = jnp.zeros((8, LANES), f32), jnp.zeros((8, LANES), f32)
        for s in range(4):
            moved = masked_ref[s, begin : begin + frames, :]
            plain = plain + fold(ones[s] * moved)
            centred = centred + fold(offs[s] * moved)
        in_ref[tap : tap + 1, :] = squash(plain)
        off_ref[tap : tap + 1, :] = squash(centred)


def gate_kernel(conv_ref, back_ref, masked_ref, stats_ref, hidden_ref, grad_ref, sums_ref):
    span = conv_ref.shape[1]
    frames = span - 2 * EDGE
    gain_sum, bias_sum = jnp.zeros((8, LANES), f32), jnp.zeros((8, LANES), f32)
    for s in range(4):
        standard = (conv_ref[s] - stats_ref[0:1, :]) * stats_ref[1:2, :]
        scaled = stats_ref[2:3, :] * standard + stats_ref[3:4, :]
        logistic = jax.nn.sigmoid(scaled)
        hidden = scaled * logistic
        hidden_ref[s] = hidden[EDGE : EDGE + frames].astype(bf16)
        grad = back_ref[s] * logistic * (1.0 + scaled * (1.0 - logistic))
        grad_ref[s] = grad
        inner = grad[EDGE : EDGE + frames]
        gain_sum = gain_sum + fold(inner * standard[EDGE : EDGE + frames])
        bias_sum = bias_sum + fold(inner)
    for tap in range(KERNEL):
        begin = HALO - HALF + tap
        acc = jnp.zeros((8, LANES), f32)
        for s in range(4):
            acc = acc + fold(grad_ref[s, EDGE : EDGE + frames, :] * masked_ref[s, begin : begin + frames, :])
        sums_ref[tap : tap + 1, :] = squash(acc)
    sums_ref[KERNEL : KERNEL + 1, :] = squash(gain_sum)
    sums_ref[KERNEL + 1 : KERNEL + 2, :] = squash(bias_sum)
    sums_ref[KERNEL + 2 : KERNEL + 3, :] = jnp.zeros((1, LANES), f32)


def by_lanes(kernel, ins, outs, scratch=(), meta=None):
    def spec(array):
        lead = array.shape[:-1]
        return pl.BlockSpec(lead + (LANES,), lambda i, *_: (0,) * len(lead) + (i,))

    shapes = [jax.ShapeDtypeStruct(shape, dtype) for shape, dtype in outs]
    prefetch = [] if meta is None else [meta]
    return pl.pallas_call(
        kernel,
        out_shape=shapes,
        grid_spec=pltpu.PrefetchScalarGridSpec(
            num_scalar_prefetch=len(prefetch),
            grid=(ins[0].shape[-1] // LANES,),
            in_specs=[spec(x) for x in ins],
            out_specs=[spec(x) for x in shapes],
            scratch_shapes=list(scratch),
        ),
        compiler_params=pltpu.CompilerParams(vmem_limit_bytes=VMEM_LIMIT),
    )(*prefetch, *ins)


def on_device(
    glu_out, lengths, kernel, gain, bias, weight, master, moment_one, moment_two, cotangent
):
    frames, width = glu_out.shape[1:]
    dp = lax.axis_index(DP)
    seq = lax.axis_index(SEQ)
    own = width // 4

    glu_out, cotangent = glu_out[0], cotangent[0]
    below = jnp.concatenate([glu_out[frames - HALO :], cotangent[frames - EDGE :]])
    above = jnp.concatenate([glu_out[:HALO], cotangent[:EDGE]])
    below, above, weight = barrier((below, above, weight))
    low, high = shift(below, SEQ, 1), shift(above, SEQ, -1)
    rows = exchange(weight, "x")
    low, high, rows, lengths, kernel, gain, bias = barrier(
        (low, high, rows, lengths, kernel, gain, bias)
    )
    cot = jnp.concatenate([low[HALO:], cotangent, high[HALO:]], axis=0)
    cot_z = swap(cot, "zl", 1)
    slab = jnp.concatenate([low[:HALO], glu_out, high[:HALO]], axis=0)
    pick = lambda m: lax.dynamic_slice_in_dim(slab, (dp ^ m) * own, own, axis=1)
    slabs = jnp.stack([pick(0)] + [swap(pick(m), DP, m) for m in (1, 2, 3)])
    count = jnp.sum(lengths).astype(f32)
    places = jnp.arange(4, dtype=jnp.int32)
    limit = jnp.sum(jnp.where(places[None, :] == (dp ^ places)[:, None], lengths, 0), axis=1)

    rows = jnp.concatenate(in_order(lax.axis_index("x"), rows), axis=0)
    rows, limit = barrier((rows, limit))
    rows = jnp.stack(in_order(lax.axis_index("zh"), exchange(rows, "zh")), axis=0)
    slabs, rows = barrier((slabs, rows))
    rows = jnp.stack(in_order(lax.axis_index("y"), exchange(rows, "y")), axis=1).reshape(own, width)

    def valid_rows(extra):
        positions = seq * frames - extra + jnp.arange(frames + 2 * extra, dtype=jnp.int32)
        return ((positions >= 0) & (positions < limit[:, None]))[:, :, None]

    def mine(table):
        return lax.dynamic_slice_in_dim(table, dp * own, own, axis=table.ndim - 1)

    taps, gain_own, bias_own = mine(kernel), mine(gain), mine(bias)

    span = frames + 2 * EDGE
    meta = jnp.concatenate([limit, jnp.full((1,), seq, jnp.int32)])
    masked, conv_out, stats = by_lanes(
        conv_kernel,
        [slabs, taps],
        [((4, frames + 2 * HALO, own), f32), ((4, span, own), f32), ((3, own), f32)],
        meta=meta,
    )
    mean = stats[1]
    stats, rows, cot_z = barrier((stats, rows, cot_z))

    pair = swap(jnp.stack([cot, cot_z]), "core", 1)
    grad_out = jnp.stack([cot, pair[0], cot_z, pair[1]])
    grad_out = jnp.where(valid_rows(EDGE), grad_out, jnp.zeros((), bf16))
    hidden_grad = lax.dot_general(
        grad_out.reshape(4 * span, width), rows, (((1,), (1,)), ((), ())), preferred_element_type=f32
    ).reshape(4, span, own)

    tap_in, tap_off = by_lanes(
        moment_kernel,
        [masked, conv_out, stats],
        [((KERNEL, own), f32)] * 2,
        [pltpu.VMEM((4, frames, LANES), f32)] * 2,
        meta=meta,
    )
    for axis, mask in STAGES[:4]:
        stats = combine(stats, axis, mask)
    stats, hidden_grad, tap_in, tap_off = barrier((stats, hidden_grad, tap_in, tap_off))
    for axis, mask in STAGES[4:]:
        stats = combine(stats, axis, mask)
    channel_mean = stats[1]
    inv_std = lax.rsqrt(stats[2] / count + norm_eps)
    tap_pair = jnp.stack([tap_in, inv_std * (tap_off + (mean - channel_mean) * tap_in)])

    hidden, scaled_grad, sums = by_lanes(
        gate_kernel,
        [conv_out, hidden_grad, masked, jnp.stack([channel_mean, inv_std, gain_own, bias_own])],
        [((4, frames, own), bf16), ((4, span, own), f32), ((KERNEL + 3, own), f32)],
    )

    flat = hidden.reshape(4 * frames, own)
    weight_grad = lax.dot_general(
        flat,
        grad_out[:, EDGE : EDGE + frames].reshape(4 * frames, width),
        (((0,), (0,)), ((), ())),
        preferred_element_type=f32,
    ).reshape(4, 4, own // 16, width)
    product = jnp.dot(flat, rows, preferred_element_type=f32).reshape(4, frames, width)

    weight_grad, sums = scatter_stage(weight_grad, sums, "y", 1)
    other = swap(jnp.stack([product[1], product[3]]).astype(bf16), "core", 1).astype(f32)
    kept, far = product[0] + other[0], product[2] + other[1]
    for axis, mask in STAGES[:3]:
        tap_pair = tap_pair + swap(tap_pair, axis, mask)
    weight_grad, sums, kept, far, tap_pair = barrier((weight_grad, sums, kept, far, tap_pair))
    weight_grad, sums = scatter_stage(weight_grad, sums, "zh", 0)
    product = kept + swap(far.astype(bf16), "zl", 1).astype(f32)
    for axis, mask in STAGES[3:]:
        tap_pair = tap_pair + swap(tap_pair, axis, mask)
    weight_grad, sums = scatter_stage(weight_grad.reshape(4, own // 64, width), sums, "x", 0)
    stream_valid = (seq * frames + jnp.arange(frames, dtype=jnp.int32) < limit[0])[:, None]
    module_out = jnp.where(stream_valid, product, 0.0).astype(bf16)
    gain_grad, bias_grad = sums[KERNEL], sums[KERNEL + 1]

    standard = (conv_out - channel_mean) * inv_std
    conv_grad = jnp.where(
        valid_rows(EDGE),
        inv_std
        * (
            gain_own * scaled_grad
            - gain_own * bias_grad / count
            - standard * gain_own * gain_grad / count
        ),
        0.0,
    )
    flipped = jnp.zeros((4, frames, own), f32)
    for tap in range(KERNEL):
        begin = EDGE + HALF - tap
        flipped = flipped + taps[tap] * conv_grad[:, begin : begin + frames]
    flipped = jnp.where(valid_rows(0), flipped, 0.0).astype(bf16)
    tap_sums = (inv_std * gain_own) * (
        sums[:KERNEL] - bias_grad / count * tap_pair[0] - gain_grad / count * tap_pair[1]
    )
    table = jnp.concatenate([tap_sums, sums[KERNEL : KERNEL + 2]], axis=0)
    parts = [flipped[0]] + [swap(flipped[m], DP, m) for m in (1, 2, 3)]
    input_grad = jnp.concatenate(in_order(dp, parts), axis=1)
    table = jnp.concatenate(in_order(dp, exchange(table, DP)), axis=1)

    new_one = beta_one * moment_one + (1.0 - beta_one) * weight_grad
    new_two = beta_two * moment_two + (1.0 - beta_two) * weight_grad * weight_grad
    new_master = master - adam_rate * (new_one / first_fix) / (
        jnp.sqrt(new_two / second_fix) + adam_eps
    )
    return (
        module_out[None],
        input_grad[None],
        table[:KERNEL],
        table[KERNEL],
        table[KERNEL + 1],
        new_master,
        new_one,
        new_two,
    )


def solution(mesh):
    fine = Mesh(mesh.devices.reshape(2, 2, 4, 4, 4), DP + SEQ)
    whole, split, tall = P(), P(DP, SEQ, None), P(DP + SEQ, None)
    return jax.shard_map(
        on_device,
        mesh=fine,
        in_specs=(split, whole, whole, whole, whole, tall, tall, tall, tall, split),
        out_specs=(split, split, whole, whole, whole, tall, tall, tall),
        check_vma=False,
    )
```

```python
import jax
import jax.numpy as jnp
from jax import lax
from jax.experimental import pallas as pl
from jax.experimental.pallas import tpu as pltpu
from jax.sharding import Mesh, PartitionSpec as P

KERNEL = 31
HALF = 15
HALO = 32
EDGE = 16

beta_one = 0.9
beta_two = 0.999
adam_rate = 0.001
adam_eps = 1e-08
norm_eps = 1e-05
first_fix = 0.9999734386011124
second_fix = 0.09520785288629043

SEQ = ("zh", "y", "x")
DP = ("zl", "core")
f32 = jnp.float32
bf16 = jnp.bfloat16


def size(axis):
    return lax.axis_size(axis)


def swap(value, axis, mask):
    return lax.ppermute(value, axis, [(i, i ^ mask) for i in range(size(axis))])


def shift(value, axis, step):
    count = size(axis)
    return lax.ppermute(value, axis, [(i, (i + step) % count) for i in range(count)])


def in_order(index, parts):
    odd, high = (index & 1) == 1, (index & 2) == 2
    r0, r1, r2, r3 = parts
    a, b = jnp.where(odd, r1, r0), jnp.where(odd, r0, r1)
    c, d = jnp.where(odd, r3, r2), jnp.where(odd, r2, r3)
    return (jnp.where(high, c, a), jnp.where(high, d, b), jnp.where(high, a, c), jnp.where(high, b, d))


def exchange(value, axis):
    return [value] + [swap(value, axis, m) for m in (1, 2, 3)]


barrier = lax.optimization_barrier
STAGES = (("x", 1), ("x", 2), ("zh", 1), ("zh", 2), ("y", 1), ("y", 2))


def halves(value):
    high = lax.reduce_precision(value, 8, 7)
    low = lax.reduce_precision(value - high, 8, 7)
    cut = value.shape[0] // 2
    parts = [high[:cut], high[cut:], low[:cut], low[cut:]]
    return jnp.concatenate(parts, axis=1).astype(bf16)


def whole_again(rows):
    width = rows.shape[1] // 4
    parts = [rows[:, k * width : (k + 1) * width].astype(f32) for k in range(4)]
    return jnp.concatenate([parts[0] + parts[2], parts[1] + parts[3]], axis=0)


def four(parts):
    return (parts[0] + parts[1]) + (parts[2] + parts[3])


def scatter_stage(value, side, axis, dim):
    me = lax.axis_index(axis)
    width = value.shape[-1]
    packed = halves(side)
    blocks = [lax.dynamic_index_in_dim(value, me ^ m, dim, keepdims=False) for m in range(4)]
    kept, sides = [blocks[0]], [whole_again(packed)]
    for m in (1, 2, 3):
        message = jnp.concatenate([blocks[m].astype(bf16).reshape(-1, width), packed], axis=0)
        message = swap(message, axis, m)
        cut = message.shape[0] - packed.shape[0]
        kept.append(message[:cut].astype(f32).reshape(blocks[0].shape))
        sides.append(whole_again(message[cut:]))
    return four(kept), four(sides)


def combine(stats, axis, mask):
    other = swap(stats, axis, mask)
    n = stats[0:1] + other[0:1]
    mean = (stats[0:1] * stats[1:2] + other[0:1] * other[1:2]) / jnp.maximum(n, 1.0)
    here, there = stats[1:2] - mean, other[1:2] - mean
    spread = stats[2:3] + other[2:3] + stats[0:1] * here * here + other[0:1] * there * there
    return jnp.concatenate([n, mean, spread])


LANES = 128
VMEM_LIMIT = 40 * 1024 * 1024


def valid_in(meta_ref, stream, frames, extra):
    rows = frames + 2 * extra
    place = lax.broadcasted_iota(jnp.int32, (rows, LANES), 0) + (meta_ref[4] * frames - extra)
    return (place >= 0) & (place < meta_ref[stream])


def fold(rows):
    return jnp.sum(rows.reshape(-1, 8, LANES), axis=0)


def squash(rows):
    return jnp.sum(rows, axis=0, keepdims=True)


def conv_kernel(meta_ref, slab_ref, taps_ref, masked_ref, conv_ref, stats_ref):
    span = conv_ref.shape[1]
    frames = span - 2 * EDGE
    half = span // 2
    n = jnp.int32(0)
    total = jnp.zeros((8, LANES), f32)
    for s in range(4):
        n = n + jnp.clip(meta_ref[s] - meta_ref[4] * frames, 0, frames)
        slab = slab_ref[s].astype(f32)
        masked_ref[s] = jnp.where(valid_in(meta_ref, s, frames, HALO), slab, 0.0)
        for part in range(2):
            acc = jnp.zeros((half, LANES), f32)
            for tap in range(KERNEL):
                begin = HALO - EDGE - HALF + tap + part * half
                acc = acc + taps_ref[tap : tap + 1, :] * masked_ref[s, begin : begin + half, :]
            conv_ref[s, part * half : (part + 1) * half, :] = acc
        inner = conv_ref[s, EDGE : EDGE + frames, :]
        total = total + fold(jnp.where(valid_in(meta_ref, s, frames, 0), inner, 0.0))
    number = jnp.full((1, LANES), n, jnp.int32).astype(f32)
    mean = squash(total) / jnp.maximum(number, 1.0)
    spread = jnp.zeros((8, LANES), f32)
    for s in range(4):
        off = conv_ref[s, EDGE : EDGE + frames, :] - mean
        off = jnp.where(valid_in(meta_ref, s, frames, 0), off, 0.0)
        spread = spread + fold(off * off)
    stats_ref[0:1, :] = number
    stats_ref[1:2, :] = mean
    stats_ref[2:3, :] = squash(spread)


def moment_kernel(meta_ref, masked_ref, conv_ref, mean_ref, in_ref, off_ref, ones, offs):
    frames = ones.shape[1]
    for s in range(4):
        valid = valid_in(meta_ref, s, frames, 0)
        ones[s] = jnp.where(valid, 1.0, 0.0)
        offs[s] = jnp.where(valid, conv_ref[s, EDGE : EDGE + frames, :] - mean_ref[...], 0.0)
    for tap in range(KERNEL):
        begin = HALO - HALF + tap
        plain, centred = jnp.zeros((8, LANES), f32), jnp.zeros((8, LANES), f32)
        for s in range(4):
            moved = masked_ref[s, begin : begin + frames, :]
            plain = plain + fold(ones[s] * moved)
            centred = centred + fold(offs[s] * moved)
        in_ref[tap : tap + 1, :] = squash(plain)
        off_ref[tap : tap + 1, :] = squash(centred)


def gate_kernel(meta_ref, conv_ref, back_ref, masked_ref, stats_ref, affine_ref, hidden_ref, grad_ref, sums_ref):
    count = jnp.full((1, LANES), meta_ref[5], jnp.int32).astype(f32)
    inv_std = lax.rsqrt(stats_ref[2:3, :] / count + norm_eps)
    span = conv_ref.shape[1]
    frames = span - 2 * EDGE
    gain_sum, bias_sum = jnp.zeros((8, LANES), f32), jnp.zeros((8, LANES), f32)
    for s in range(4):
        standard = (conv_ref[s] - stats_ref[1:2, :]) * inv_std
        scaled = affine_ref[0:1, :] * standard + affine_ref[1:2, :]
        logistic = jax.nn.sigmoid(scaled)
        hidden = scaled * logistic
        hidden_ref[s] = hidden[EDGE : EDGE + frames].astype(bf16)
        grad = back_ref[s] * logistic * (1.0 + scaled * (1.0 - logistic))
        grad_ref[s] = grad
        inner = grad[EDGE : EDGE + frames]
        gain_sum = gain_sum + fold(inner * standard[EDGE : EDGE + frames])
        bias_sum = bias_sum + fold(inner)
    for tap in range(KERNEL):
        begin = HALO - HALF + tap
        acc = jnp.zeros((8, LANES), f32)
        for s in range(4):
            acc = acc + fold(grad_ref[s, EDGE : EDGE + frames, :] * masked_ref[s, begin : begin + frames, :])
        sums_ref[tap : tap + 1, :] = squash(acc)
    sums_ref[KERNEL : KERNEL + 1, :] = squash(gain_sum)
    sums_ref[KERNEL + 1 : KERNEL + 2, :] = squash(bias_sum)
    sums_ref[KERNEL + 2 : KERNEL + 3, :] = jnp.zeros((1, LANES), f32)


def input_kernel(meta_ref, conv_ref, grad_ref, stats_ref, affine_ref, sums_ref, taps_ref, out_ref, back):
    span = conv_ref.shape[1]
    frames = span - 2 * EDGE
    count = jnp.full((1, LANES), meta_ref[5], jnp.int32).astype(f32)
    inv_std = lax.rsqrt(stats_ref[2:3, :] / count + norm_eps)
    gain = affine_ref[0:1, :]
    gain_part = gain * sums_ref[KERNEL : KERNEL + 1, :] / count
    bias_part = gain * sums_ref[KERNEL + 1 : KERNEL + 2, :] / count
    for s in range(4):
        standard = (conv_ref[s] - stats_ref[1:2, :]) * inv_std
        grad = inv_std * (gain * grad_ref[s] - bias_part - standard * gain_part)
        back[s] = jnp.where(valid_in(meta_ref, s, frames, EDGE), grad, 0.0)
        valid = valid_in(meta_ref, s, frames, 0)
        half = frames // 2
        for part in range(2):
            acc = jnp.zeros((half, LANES), f32)
            for tap in range(KERNEL):
                begin = EDGE + HALF - tap + part * half
                acc = acc + taps_ref[tap : tap + 1, :] * back[s, begin : begin + half, :]
            rows = slice(part * half, (part + 1) * half)
            out_ref[s, rows, :] = jnp.where(valid[rows], acc, 0.0).astype(bf16)


def by_lanes(kernel, ins, outs, scratch=(), meta=None):
    def spec(array):
        lead = array.shape[:-1]
        return pl.BlockSpec(lead + (LANES,), lambda i, *_: (0,) * len(lead) + (i,))

    shapes = [jax.ShapeDtypeStruct(shape, dtype) for shape, dtype in outs]
    prefetch = [] if meta is None else [meta]
    return pl.pallas_call(
        kernel,
        out_shape=shapes,
        grid_spec=pltpu.PrefetchScalarGridSpec(
            num_scalar_prefetch=len(prefetch),
            grid=(ins[0].shape[-1] // LANES,),
            in_specs=[spec(x) for x in ins],
            out_specs=[spec(x) for x in shapes],
            scratch_shapes=list(scratch),
        ),
        compiler_params=pltpu.CompilerParams(vmem_limit_bytes=VMEM_LIMIT),
    )(*prefetch, *ins)


def on_device(
    glu_out, lengths, kernel, gain, bias, weight, master, moment_one, moment_two, cotangent
):
    frames, width = glu_out.shape[1:]
    dp = lax.axis_index(DP)
    seq = lax.axis_index(SEQ)
    own = width // 4

    glu_out, cotangent = glu_out[0], cotangent[0]
    below = jnp.concatenate([glu_out[frames - HALO :], cotangent[frames - EDGE :]])
    above = jnp.concatenate([glu_out[:HALO], cotangent[:EDGE]])
    below, above, weight = barrier((below, above, weight))
    low, high = shift(below, SEQ, 1), shift(above, SEQ, -1)
    rows = exchange(weight, "x")
    low, high, rows, lengths, kernel, gain, bias = barrier(
        (low, high, rows, lengths, kernel, gain, bias)
    )
    cot = jnp.concatenate([low[HALO:], cotangent, high[HALO:]], axis=0)
    cot_z = swap(cot, "zl", 1)
    slab = jnp.concatenate([low[:HALO], glu_out, high[:HALO]], axis=0)
    pick = lambda m: lax.dynamic_slice_in_dim(slab, (dp ^ m) * own, own, axis=1)
    pieces = [pick(0)] + [swap(pick(m), DP, m) for m in (1, 2, 3)]
    total = jnp.sum(lengths)
    count = total.astype(f32)
    places = jnp.arange(4, dtype=jnp.int32)
    limit = jnp.sum(jnp.where(places[None, :] == (dp ^ places)[:, None], lengths, 0), axis=1)
    meta = jnp.concatenate([limit, jnp.stack([seq, total])])

    rows, pieces[2] = barrier((rows, pieces[2]))
    rows = jnp.concatenate(in_order(lax.axis_index("x"), rows), axis=0)
    rows = jnp.stack(in_order(lax.axis_index("zh"), exchange(rows, "zh")), axis=0)
    slabs = jnp.stack(pieces)
    slabs, meta = barrier((slabs, meta))

    def valid_rows(extra):
        positions = seq * frames - extra + jnp.arange(frames + 2 * extra, dtype=jnp.int32)
        return ((positions >= 0) & (positions < limit[:, None]))[:, :, None]

    def mine(table):
        return lax.dynamic_slice_in_dim(table, dp * own, own, axis=table.ndim - 1)

    taps, affine = mine(kernel), mine(jnp.stack([gain, bias]))
    gain_own = affine[0:1]

    span = frames + 2 * EDGE
    masked, conv_out, stats = by_lanes(
        conv_kernel,
        [slabs, taps],
        [((4, frames + 2 * HALO, own), f32), ((4, span, own), f32), ((3, own), f32)],
        meta=meta,
    )
    mean = stats[1:2]
    stats, cot_z, affine = barrier((stats, cot_z, affine))

    pair = swap(jnp.stack([cot, cot_z]), "core", 1)
    stats = combine(stats, *STAGES[0])
    stats, rows, mean, pair = barrier((stats, rows, mean, pair))
    rows = jnp.stack(in_order(lax.axis_index("y"), exchange(rows, "y")), axis=1).reshape(own, width)
    grad_out = jnp.stack([cot, pair[0], cot_z, pair[1]])
    grad_out = jnp.where(valid_rows(EDGE), grad_out, jnp.zeros((), bf16))
    hidden_grad = lax.dot_general(
        grad_out.reshape(4 * span, width), rows, (((1,), (1,)), ((), ())), preferred_element_type=f32
    ).reshape(4, span, own)

    tap_in, tap_off = by_lanes(
        moment_kernel,
        [masked, conv_out, mean],
        [((KERNEL, own), f32)] * 2,
        [pltpu.VMEM((4, frames, LANES), f32)] * 2,
        meta=meta,
    )
    for axis, mask in STAGES[1:4]:
        stats = combine(stats, axis, mask)
    grad_inner = grad_out[:, EDGE : EDGE + frames].reshape(4 * frames, width)
    stats, hidden_grad, tap_in, tap_off, grad_inner = barrier(
        (stats, hidden_grad, tap_in, tap_off, grad_inner)
    )
    for axis, mask in STAGES[4:]:
        stats = combine(stats, axis, mask)

    hidden, scaled_grad, sums = by_lanes(
        gate_kernel,
        [conv_out, hidden_grad, masked, stats, affine],
        [((4, frames, own), bf16), ((4, span, own), f32), ((KERNEL + 3, own), f32)],
        meta=meta,
    )
    stats, tap_in, tap_off, sums = barrier((stats, tap_in, tap_off, sums))
    channel_mean = stats[1:2]
    inv_std = lax.rsqrt(stats[2:3] / count + norm_eps)
    tap_pair = jnp.stack([tap_in, inv_std * (tap_off + (mean - channel_mean) * tap_in)])

    flat = hidden.reshape(4 * frames, own)
    weight_grad = lax.dot_general(
        flat,
        grad_inner,
        (((0,), (0,)), ((), ())),
        preferred_element_type=f32,
    ).reshape(4, 4, own // 16, width)
    product = jnp.dot(flat, rows, preferred_element_type=f32).reshape(4, frames, width)

    weight_grad, sums = scatter_stage(weight_grad, sums, "y", 1)
    other = swap(jnp.stack([product[1], product[3]]).astype(bf16), "core", 1).astype(f32)
    kept, far = product[0] + other[0], product[2] + other[1]
    product = kept + swap(far.astype(bf16), "zl", 1).astype(f32)
    for axis, mask in STAGES[:3]:
        tap_pair = tap_pair + swap(tap_pair, axis, mask)
    weight_grad, sums, tap_pair, product = barrier((weight_grad, sums, tap_pair, product))
    weight_grad, sums = scatter_stage(weight_grad, sums, "zh", 0)
    for axis, mask in STAGES[4:]:
        tap_pair = tap_pair + swap(tap_pair, axis, mask)
    weight_grad, sums, tap_pair = barrier((weight_grad, sums, tap_pair))
    weight_grad, sums = scatter_stage(weight_grad.reshape(4, own // 64, width), sums, "x", 0)
    for axis, mask in STAGES[3:4]:
        tap_pair = tap_pair + swap(tap_pair, axis, mask)
    stream_valid = (seq * frames + jnp.arange(frames, dtype=jnp.int32) < limit[0])[:, None]
    module_out = jnp.where(stream_valid, product, 0.0).astype(bf16)

    (flipped,) = by_lanes(
        input_kernel,
        [conv_out, scaled_grad, stats, affine, sums, taps],
        [((4, frames, own), bf16)],
        [pltpu.VMEM((4, span, LANES), f32)],
        meta=meta,
    )
    _, sums = barrier((flipped, sums))
    gain_grad, bias_grad = sums[KERNEL : KERNEL + 1], sums[KERNEL + 1 : KERNEL + 2]
    tap_sums = (inv_std * gain_own) * (
        sums[:KERNEL] - bias_grad / count * tap_pair[0] - gain_grad / count * tap_pair[1]
    )
    table = jnp.concatenate([tap_sums, sums[KERNEL : KERNEL + 2]], axis=0)
    parts = [flipped[0]] + [swap(flipped[m], DP, m) for m in (1, 2, 3)]
    input_grad = jnp.concatenate(in_order(dp, parts), axis=1)
    table = jnp.concatenate(in_order(dp, exchange(table, DP)), axis=1)

    new_one = beta_one * moment_one + (1.0 - beta_one) * weight_grad
    new_two = beta_two * moment_two + (1.0 - beta_two) * weight_grad * weight_grad
    new_master = master - adam_rate * (new_one / first_fix) / (
        jnp.sqrt(new_two / second_fix) + adam_eps
    )
    return (
        module_out[None],
        input_grad[None],
        table[:KERNEL],
        table[KERNEL],
        table[KERNEL + 1],
        new_master,
        new_one,
        new_two,
    )


def solution(mesh):
    fine = Mesh(mesh.devices.reshape(2, 2, 4, 4, 4), DP + SEQ)
    whole, split, tall = P(), P(DP, SEQ, None), P(DP + SEQ, None)
    return jax.shard_map(
        on_device,
        mesh=fine,
        in_specs=(split, whole, whole, whole, whole, tall, tall, tall, tall, split),
        out_specs=(split, split, whole, whole, whole, tall, tall, tall),
        check_vma=False,
    )
```

```python
import jax
import jax.numpy as jnp
from jax import lax
from jax.experimental import pallas as pl
from jax.experimental.pallas import tpu as pltpu
from jax.sharding import Mesh, PartitionSpec as P

KERNEL = 31
HALF = 15
HALO = 32
EDGE = 16

beta_one = 0.9
beta_two = 0.999
adam_rate = 0.001
adam_eps = 1e-08
norm_eps = 1e-05
first_fix = 0.9999734386011124
second_fix = 0.09520785288629043

SEQ = ("zh", "y", "x")
DP = ("zl", "core")
f32 = jnp.float32
bf16 = jnp.bfloat16


def size(axis):
    return lax.axis_size(axis)


def swap(value, axis, mask):
    return lax.ppermute(value, axis, [(i, i ^ mask) for i in range(size(axis))])


def shift(value, axis, step):
    count = size(axis)
    return lax.ppermute(value, axis, [(i, (i + step) % count) for i in range(count)])


def in_order(index, parts):
    odd, high = (index & 1) == 1, (index & 2) == 2
    r0, r1, r2, r3 = parts
    a, b = jnp.where(odd, r1, r0), jnp.where(odd, r0, r1)
    c, d = jnp.where(odd, r3, r2), jnp.where(odd, r2, r3)
    return (jnp.where(high, c, a), jnp.where(high, d, b), jnp.where(high, a, c), jnp.where(high, b, d))


def exchange(value, axis):
    return [value] + [swap(value, axis, m) for m in (1, 2, 3)]


barrier = lax.optimization_barrier
STAGES = (("x", 1), ("x", 2), ("zh", 1), ("zh", 2), ("y", 1), ("y", 2))


def side_by_side(table, axis):
    other = swap(table, axis, 1)
    second = lax.axis_index(axis) == 1
    parts = [jnp.where(second, other, table), jnp.where(second, table, other)]
    return jnp.concatenate(parts, axis=1)


def halves(value):
    high = lax.reduce_precision(value, 8, 7)
    low = lax.reduce_precision(value - high, 8, 7)
    cut = value.shape[0] // 2
    parts = [high[:cut], high[cut:], low[:cut], low[cut:]]
    return jnp.concatenate(parts, axis=1).astype(bf16)


def whole_again(rows):
    width = rows.shape[1] // 4
    parts = [rows[:, k * width : (k + 1) * width].astype(f32) for k in range(4)]
    return jnp.concatenate([parts[0] + parts[2], parts[1] + parts[3]], axis=0)


def four(parts):
    return (parts[0] + parts[1]) + (parts[2] + parts[3])


def scatter_stage(value, side, axis, dim):
    me = lax.axis_index(axis)
    width = value.shape[-1]
    packed = halves(side)
    blocks = [lax.dynamic_index_in_dim(value, me ^ m, dim, keepdims=False) for m in range(4)]
    kept, sides = [blocks[0]], [whole_again(packed)]
    for m in (1, 2, 3):
        message = jnp.concatenate([blocks[m].astype(bf16).reshape(-1, width), packed], axis=0)
        message = swap(message, axis, m)
        cut = message.shape[0] - packed.shape[0]
        kept.append(message[:cut].astype(f32).reshape(blocks[0].shape))
        sides.append(whole_again(message[cut:]))
    return four(kept), four(sides)


def combine(stats, axis, mask):
    other = swap(stats, axis, mask)
    n = stats[0:1] + other[0:1]
    mean = (stats[0:1] * stats[1:2] + other[0:1] * other[1:2]) / jnp.maximum(n, 1.0)
    here, there = stats[1:2] - mean, other[1:2] - mean
    spread = stats[2:3] + other[2:3] + stats[0:1] * here * here + other[0:1] * there * there
    return jnp.concatenate([n, mean, spread])


LANES = 128
VMEM_LIMIT = 40 * 1024 * 1024


def valid_in(meta_ref, stream, frames, extra):
    rows = frames + 2 * extra
    place = lax.broadcasted_iota(jnp.int32, (rows, LANES), 0) + (meta_ref[4] * frames - extra)
    return (place >= 0) & (place < meta_ref[stream])


def fold(rows):
    return jnp.sum(rows.reshape(-1, 8, LANES), axis=0)


def squash(rows):
    return jnp.sum(rows, axis=0, keepdims=True)


def conv_kernel(meta_ref, slab_ref, taps_ref, masked_ref, conv_ref, stats_ref):
    span = conv_ref.shape[1]
    frames = span - 2 * EDGE
    half = span // 2
    n = jnp.int32(0)
    total = jnp.zeros((8, LANES), f32)
    for s in range(4):
        n = n + jnp.clip(meta_ref[s] - meta_ref[4] * frames, 0, frames)
        slab = slab_ref[s].astype(f32)
        masked_ref[s] = jnp.where(valid_in(meta_ref, s, frames, HALO), slab, 0.0)
        for part in range(2):
            acc = jnp.zeros((half, LANES), f32)
            for tap in range(KERNEL):
                begin = HALO - EDGE - HALF + tap + part * half
                acc = acc + taps_ref[tap : tap + 1, :] * masked_ref[s, begin : begin + half, :]
            conv_ref[s, part * half : (part + 1) * half, :] = acc
        inner = conv_ref[s, EDGE : EDGE + frames, :]
        total = total + fold(jnp.where(valid_in(meta_ref, s, frames, 0), inner, 0.0))
    number = jnp.full((1, LANES), n, jnp.int32).astype(f32)
    mean = squash(total) / jnp.maximum(number, 1.0)
    spread = jnp.zeros((8, LANES), f32)
    for s in range(4):
        off = conv_ref[s, EDGE : EDGE + frames, :] - mean
        off = jnp.where(valid_in(meta_ref, s, frames, 0), off, 0.0)
        spread = spread + fold(off * off)
    stats_ref[0:1, :] = number
    stats_ref[1:2, :] = mean
    stats_ref[2:3, :] = squash(spread)


def moment_kernel(meta_ref, masked_ref, conv_ref, mean_ref, in_ref, off_ref, ones, offs):
    frames = ones.shape[1]
    for s in range(4):
        valid = valid_in(meta_ref, s, frames, 0)
        ones[s] = jnp.where(valid, 1.0, 0.0)
        offs[s] = jnp.where(valid, conv_ref[s, EDGE : EDGE + frames, :] - mean_ref[...], 0.0)
    for tap in range(KERNEL):
        begin = HALO - HALF + tap
        plain, centred = jnp.zeros((8, LANES), f32), jnp.zeros((8, LANES), f32)
        for s in range(4):
            moved = masked_ref[s, begin : begin + frames, :]
            plain = plain + fold(ones[s] * moved)
            centred = centred + fold(offs[s] * moved)
        in_ref[tap : tap + 1, :] = squash(plain)
        off_ref[tap : tap + 1, :] = squash(centred)


def gate_kernel(meta_ref, conv_ref, back_ref, masked_ref, stats_ref, affine_ref, hidden_ref, grad_ref, sums_ref):
    count = jnp.full((1, LANES), meta_ref[5], jnp.int32).astype(f32)
    inv_std = lax.rsqrt(stats_ref[2:3, :] / count + norm_eps)
    span = conv_ref.shape[1]
    frames = span - 2 * EDGE
    gain_sum, bias_sum = jnp.zeros((8, LANES), f32), jnp.zeros((8, LANES), f32)
    for s in range(4):
        standard = (conv_ref[s] - stats_ref[1:2, :]) * inv_std
        scaled = affine_ref[0:1, :] * standard + affine_ref[1:2, :]
        logistic = jax.nn.sigmoid(scaled)
        hidden = scaled * logistic
        hidden_ref[s] = hidden[EDGE : EDGE + frames].astype(bf16)
        grad = back_ref[s] * logistic * (1.0 + scaled * (1.0 - logistic))
        grad_ref[s] = grad
        inner = grad[EDGE : EDGE + frames]
        gain_sum = gain_sum + fold(inner * standard[EDGE : EDGE + frames])
        bias_sum = bias_sum + fold(inner)
    for tap in range(KERNEL):
        begin = HALO - HALF + tap
        acc = jnp.zeros((8, LANES), f32)
        for s in range(4):
            acc = acc + fold(grad_ref[s, EDGE : EDGE + frames, :] * masked_ref[s, begin : begin + frames, :])
        sums_ref[tap : tap + 1, :] = squash(acc)
    sums_ref[KERNEL : KERNEL + 1, :] = squash(gain_sum)
    sums_ref[KERNEL + 1 : KERNEL + 2, :] = squash(bias_sum)
    sums_ref[KERNEL + 2 : KERNEL + 3, :] = jnp.zeros((1, LANES), f32)


def input_kernel(meta_ref, conv_ref, grad_ref, stats_ref, affine_ref, sums_ref, taps_ref, out_ref, back):
    span = conv_ref.shape[1]
    frames = span - 2 * EDGE
    count = jnp.full((1, LANES), meta_ref[5], jnp.int32).astype(f32)
    inv_std = lax.rsqrt(stats_ref[2:3, :] / count + norm_eps)
    gain = affine_ref[0:1, :]
    gain_part = gain * sums_ref[KERNEL : KERNEL + 1, :] / count
    bias_part = gain * sums_ref[KERNEL + 1 : KERNEL + 2, :] / count
    for s in range(4):
        standard = (conv_ref[s] - stats_ref[1:2, :]) * inv_std
        grad = inv_std * (gain * grad_ref[s] - bias_part - standard * gain_part)
        back[s] = jnp.where(valid_in(meta_ref, s, frames, EDGE), grad, 0.0)
        valid = valid_in(meta_ref, s, frames, 0)
        half = frames // 2
        for part in range(2):
            acc = jnp.zeros((half, LANES), f32)
            for tap in range(KERNEL):
                begin = EDGE + HALF - tap + part * half
                acc = acc + taps_ref[tap : tap + 1, :] * back[s, begin : begin + half, :]
            rows = slice(part * half, (part + 1) * half)
            out_ref[s, rows, :] = jnp.where(valid[rows], acc, 0.0).astype(bf16)


def by_lanes(kernel, ins, outs, scratch=(), meta=None):
    def spec(array):
        lead = array.shape[:-1]
        return pl.BlockSpec(lead + (LANES,), lambda i, *_: (0,) * len(lead) + (i,))

    shapes = [jax.ShapeDtypeStruct(shape, dtype) for shape, dtype in outs]
    prefetch = [] if meta is None else [meta]
    return pl.pallas_call(
        kernel,
        out_shape=shapes,
        grid_spec=pltpu.PrefetchScalarGridSpec(
            num_scalar_prefetch=len(prefetch),
            grid=(ins[0].shape[-1] // LANES,),
            in_specs=[spec(x) for x in ins],
            out_specs=[spec(x) for x in shapes],
            scratch_shapes=list(scratch),
        ),
        compiler_params=pltpu.CompilerParams(vmem_limit_bytes=VMEM_LIMIT),
    )(*prefetch, *ins)


def on_device(
    glu_out, lengths, kernel, gain, bias, weight, master, moment_one, moment_two, cotangent
):
    frames, width = glu_out.shape[1:]
    dp = lax.axis_index(DP)
    seq = lax.axis_index(SEQ)
    own = width // 4

    glu_out, cotangent = glu_out[0], cotangent[0]
    below = jnp.concatenate([glu_out[frames - HALO :], cotangent[frames - EDGE :]])
    above = jnp.concatenate([glu_out[:HALO], cotangent[:EDGE]])
    below, above, weight = barrier((below, above, weight))
    low, high = shift(below, SEQ, 1), shift(above, SEQ, -1)
    rows = exchange(weight, "x")
    low, high, rows, lengths, kernel, gain, bias = barrier(
        (low, high, rows, lengths, kernel, gain, bias)
    )
    cot = jnp.concatenate([low[HALO:], cotangent, high[HALO:]], axis=0)
    cot_z = swap(cot, "zl", 1)
    slab = jnp.concatenate([low[:HALO], glu_out, high[:HALO]], axis=0)
    pick = lambda m: lax.dynamic_slice_in_dim(slab, (dp ^ m) * own, own, axis=1)
    pieces = [pick(0)] + [swap(pick(m), DP, m) for m in (1, 2, 3)]
    total = jnp.sum(lengths)
    count = total.astype(f32)
    places = jnp.arange(4, dtype=jnp.int32)
    limit = jnp.sum(jnp.where(places[None, :] == (dp ^ places)[:, None], lengths, 0), axis=1)
    meta = jnp.concatenate([limit, jnp.stack([seq, total])])

    rows, pieces[2] = barrier((rows, pieces[2]))
    rows = jnp.concatenate(in_order(lax.axis_index("x"), rows), axis=0)
    rows = jnp.stack(in_order(lax.axis_index("zh"), exchange(rows, "zh")), axis=0)
    slabs = jnp.stack(pieces)
    slabs, meta = barrier((slabs, meta))

    def valid_rows(extra):
        positions = seq * frames - extra + jnp.arange(frames + 2 * extra, dtype=jnp.int32)
        return ((positions >= 0) & (positions < limit[:, None]))[:, :, None]

    def mine(table):
        return lax.dynamic_slice_in_dim(table, dp * own, own, axis=table.ndim - 1)

    taps, affine = mine(kernel), mine(jnp.stack([gain, bias]))
    gain_own = affine[0:1]

    span = frames + 2 * EDGE
    masked, conv_out, stats = by_lanes(
        conv_kernel,
        [slabs, taps],
        [((4, frames + 2 * HALO, own), f32), ((4, span, own), f32), ((3, own), f32)],
        meta=meta,
    )
    mean = stats[1:2]
    stats, cot_z, affine = barrier((stats, cot_z, affine))

    pair = swap(jnp.stack([cot, cot_z]), "core", 1)
    stats = combine(stats, *STAGES[0])
    stats, rows, mean, pair = barrier((stats, rows, mean, pair))
    rows = jnp.stack(in_order(lax.axis_index("y"), exchange(rows, "y")), axis=1).reshape(own, width)
    grad_out = jnp.stack([cot, pair[0], cot_z, pair[1]])
    grad_out = jnp.where(valid_rows(EDGE), grad_out, jnp.zeros((), bf16))
    hidden_grad = lax.dot_general(
        grad_out.reshape(4 * span, width), rows, (((1,), (1,)), ((), ())), preferred_element_type=f32
    ).reshape(4, span, own)

    tap_in, tap_off = by_lanes(
        moment_kernel,
        [masked, conv_out, mean],
        [((KERNEL, own), f32)] * 2,
        [pltpu.VMEM((4, frames, LANES), f32)] * 2,
        meta=meta,
    )
    for axis, mask in STAGES[1:4]:
        stats = combine(stats, axis, mask)
    grad_inner = grad_out[:, EDGE : EDGE + frames].reshape(4 * frames, width)
    stats, hidden_grad, tap_in, tap_off, grad_inner = barrier(
        (stats, hidden_grad, tap_in, tap_off, grad_inner)
    )
    for axis, mask in STAGES[4:]:
        stats = combine(stats, axis, mask)

    hidden, scaled_grad, sums = by_lanes(
        gate_kernel,
        [conv_out, hidden_grad, masked, stats, affine],
        [((4, frames, own), bf16), ((4, span, own), f32), ((KERNEL + 3, own), f32)],
        meta=meta,
    )
    channel_mean = stats[1:2]
    inv_std = lax.rsqrt(stats[2:3] / count + norm_eps)
    tap_off = inv_std * (tap_off + (mean - channel_mean) * tap_in)
    sums = jnp.concatenate([sums, tap_in, tap_off])

    flat = hidden.reshape(4 * frames, own)
    weight_grad = lax.dot_general(
        flat,
        grad_inner,
        (((0,), (0,)), ((), ())),
        preferred_element_type=f32,
    ).reshape(4, 4, own // 16, width)
    product = jnp.dot(flat, rows, preferred_element_type=f32).reshape(4, frames, width)

    weight_grad, sums = scatter_stage(weight_grad, sums, "y", 1)
    other = swap(jnp.stack([product[1], product[3]]).astype(bf16), "core", 1).astype(f32)
    kept, far = product[0] + other[0], product[2] + other[1]
    product = kept + swap(far.astype(bf16), "zl", 1).astype(f32)
    weight_grad, sums, product = barrier((weight_grad, sums, product))
    weight_grad, sums = scatter_stage(weight_grad, sums, "zh", 0)
    weight_grad, sums = scatter_stage(weight_grad.reshape(4, own // 64, width), sums, "x", 0)
    stream_valid = (seq * frames + jnp.arange(frames, dtype=jnp.int32) < limit[0])[:, None]
    module_out = jnp.where(stream_valid, product, 0.0).astype(bf16)

    (flipped,) = by_lanes(
        input_kernel,
        [conv_out, scaled_grad, stats, affine, sums, taps],
        [((4, frames, own), bf16)],
        [pltpu.VMEM((4, span, LANES), f32)],
        meta=meta,
    )
    _, sums = barrier((flipped, sums))
    gain_grad, bias_grad = sums[KERNEL : KERNEL + 1], sums[KERNEL + 1 : KERNEL + 2]
    tap_in, tap_off = sums[KERNEL + 3 : 2 * KERNEL + 3], sums[2 * KERNEL + 3 :]
    tap_sums = (inv_std * gain_own) * (
        sums[:KERNEL] - bias_grad / count * tap_in - gain_grad / count * tap_off
    )
    table = jnp.concatenate([tap_sums, sums[KERNEL : KERNEL + 2]], axis=0)
    near = swap(jnp.stack([flipped[1], flipped[3]]), "core", 1)
    far = swap(jnp.stack([flipped[2], near[1]]), "zl", 1)
    input_grad = jnp.concatenate(in_order(dp, [flipped[0], near[0], far[0], far[1]]), axis=1)
    table = side_by_side(side_by_side(table, "core"), "zl")

    new_one = beta_one * moment_one + (1.0 - beta_one) * weight_grad
    new_two = beta_two * moment_two + (1.0 - beta_two) * weight_grad * weight_grad
    new_master = master - adam_rate * (new_one / first_fix) / (
        jnp.sqrt(new_two / second_fix) + adam_eps
    )
    return (
        module_out[None],
        input_grad[None],
        table[:KERNEL],
        table[KERNEL],
        table[KERNEL + 1],
        new_master,
        new_one,
        new_two,
    )


def solution(mesh):
    fine = Mesh(mesh.devices.reshape(2, 2, 4, 4, 4), DP + SEQ)
    whole, split, tall = P(), P(DP, SEQ, None), P(DP + SEQ, None)
    return jax.shard_map(
        on_device,
        mesh=fine,
        in_specs=(split, whole, whole, whole, whole, tall, tall, tall, tall, split),
        out_specs=(split, split, whole, whole, whole, tall, tall, tall),
        check_vma=False,
    )
```

```python
import jax
import jax.numpy as jnp
from jax import lax
from jax.experimental import pallas as pl
from jax.experimental.pallas import tpu as pltpu
from jax.sharding import Mesh, PartitionSpec as P

KERNEL = 31
HALF = 15
HALO = 32
EDGE = 16

beta_one = 0.9
beta_two = 0.999
adam_rate = 0.001
adam_eps = 1e-08
norm_eps = 1e-05
first_fix = 0.9999734386011124
second_fix = 0.09520785288629043

SEQ = ("zh", "y", "x")
DP = ("zl", "core")
f32 = jnp.float32
bf16 = jnp.bfloat16


def size(axis):
    return lax.axis_size(axis)


def swap(value, axis, mask):
    return lax.ppermute(value, axis, [(i, i ^ mask) for i in range(size(axis))])


def shift(value, axis, step):
    count = size(axis)
    return lax.ppermute(value, axis, [(i, (i + step) % count) for i in range(count)])


def in_order(index, parts):
    odd, high = (index & 1) == 1, (index & 2) == 2
    r0, r1, r2, r3 = parts
    a, b = jnp.where(odd, r1, r0), jnp.where(odd, r0, r1)
    c, d = jnp.where(odd, r3, r2), jnp.where(odd, r2, r3)
    return (jnp.where(high, c, a), jnp.where(high, d, b), jnp.where(high, a, c), jnp.where(high, b, d))


def exchange(value, axis):
    return [value] + [swap(value, axis, m) for m in (1, 2, 3)]


barrier = lax.optimization_barrier
STAGES = (("x", 1), ("x", 2), ("zh", 1), ("zh", 2), ("y", 1), ("y", 2))


def side_by_side(table, axis):
    other = swap(table, axis, 1)
    second = lax.axis_index(axis) == 1
    parts = [jnp.where(second, other, table), jnp.where(second, table, other)]
    return jnp.concatenate(parts, axis=1)


def halves(value):
    high = lax.reduce_precision(value, 8, 7)
    low = lax.reduce_precision(value - high, 8, 7)
    cut = value.shape[0] // 2
    parts = [high[:cut], high[cut:], low[:cut], low[cut:]]
    return jnp.concatenate(parts, axis=1).astype(bf16)


def whole_again(rows):
    width = rows.shape[1] // 4
    parts = [rows[:, k * width : (k + 1) * width].astype(f32) for k in range(4)]
    return jnp.concatenate([parts[0] + parts[2], parts[1] + parts[3]], axis=0)


def four(parts):
    return (parts[0] + parts[1]) + (parts[2] + parts[3])


def scatter_stage(value, side, axis, dim):
    me = lax.axis_index(axis)
    width = value.shape[-1]
    packed = halves(side)
    blocks = [lax.dynamic_index_in_dim(value, me ^ m, dim, keepdims=False) for m in range(4)]
    kept, sides = [blocks[0]], [whole_again(packed)]
    for m in (1, 2, 3):
        message = jnp.concatenate([blocks[m].astype(bf16).reshape(-1, width), packed], axis=0)
        message = swap(message, axis, m)
        cut = message.shape[0] - packed.shape[0]
        kept.append(message[:cut].astype(f32).reshape(blocks[0].shape))
        sides.append(whole_again(message[cut:]))
    return four(kept), four(sides)


def combine(stats, axis, mask):
    other = swap(stats, axis, mask)
    n = stats[0:1] + other[0:1]
    mean = (stats[0:1] * stats[1:2] + other[0:1] * other[1:2]) / jnp.maximum(n, 1.0)
    here, there = stats[1:2] - mean, other[1:2] - mean
    spread = stats[2:3] + other[2:3] + stats[0:1] * here * here + other[0:1] * there * there
    return jnp.concatenate([n, mean, spread])


LANES = 128
VMEM_LIMIT = 40 * 1024 * 1024


def valid_in(meta_ref, stream, frames, extra):
    rows = frames + 2 * extra
    place = lax.broadcasted_iota(jnp.int32, (rows, LANES), 0) + (meta_ref[4] * frames - extra)
    return (place >= 0) & (place < meta_ref[stream])


def fold(rows):
    return jnp.sum(rows.reshape(-1, 8, LANES), axis=0)


def squash(rows):
    return jnp.sum(rows, axis=0, keepdims=True)


def conv_kernel(meta_ref, slab_ref, taps_ref, masked_ref, conv_ref, stats_ref):
    span = conv_ref.shape[1]
    frames = span - 2 * EDGE
    half = span // 2
    n = jnp.int32(0)
    total = jnp.zeros((8, LANES), f32)
    for s in range(4):
        n = n + jnp.clip(meta_ref[s] - meta_ref[4] * frames, 0, frames)
        slab = slab_ref[s].astype(f32)
        masked_ref[s] = jnp.where(valid_in(meta_ref, s, frames, HALO), slab, 0.0)
        for part in range(2):
            acc = jnp.zeros((half, LANES), f32)
            for tap in range(KERNEL):
                begin = HALO - EDGE - HALF + tap + part * half
                acc = acc + taps_ref[tap : tap + 1, :] * masked_ref[s, begin : begin + half, :]
            conv_ref[s, part * half : (part + 1) * half, :] = acc
        inner = conv_ref[s, EDGE : EDGE + frames, :]
        total = total + fold(jnp.where(valid_in(meta_ref, s, frames, 0), inner, 0.0))
    number = jnp.full((1, LANES), n, jnp.int32).astype(f32)
    mean = squash(total) / jnp.maximum(number, 1.0)
    spread = jnp.zeros((8, LANES), f32)
    for s in range(4):
        off = conv_ref[s, EDGE : EDGE + frames, :] - mean
        off = jnp.where(valid_in(meta_ref, s, frames, 0), off, 0.0)
        spread = spread + fold(off * off)
    stats_ref[0:1, :] = number
    stats_ref[1:2, :] = mean
    stats_ref[2:3, :] = squash(spread)


def moment_kernel(meta_ref, masked_ref, conv_ref, mean_ref, in_ref, off_ref, ones, offs):
    frames = ones.shape[1]
    for s in range(4):
        valid = valid_in(meta_ref, s, frames, 0)
        ones[s] = jnp.where(valid, 1.0, 0.0)
        offs[s] = jnp.where(valid, conv_ref[s, EDGE : EDGE + frames, :] - mean_ref[...], 0.0)
    for tap in range(KERNEL):
        begin = HALO - HALF + tap
        plain, centred = jnp.zeros((8, LANES), f32), jnp.zeros((8, LANES), f32)
        for s in range(4):
            moved = masked_ref[s, begin : begin + frames, :]
            plain = plain + fold(ones[s] * moved)
            centred = centred + fold(offs[s] * moved)
        in_ref[tap : tap + 1, :] = squash(plain)
        off_ref[tap : tap + 1, :] = squash(centred)


def gate_kernel(meta_ref, conv_ref, back_ref, masked_ref, stats_ref, affine_ref, hidden_ref, grad_ref, sums_ref):
    count = jnp.full((1, LANES), meta_ref[5], jnp.int32).astype(f32)
    inv_std = lax.rsqrt(stats_ref[2:3, :] / count + norm_eps)
    span = conv_ref.shape[1]
    frames = span - 2 * EDGE
    gain_sum, bias_sum = jnp.zeros((8, LANES), f32), jnp.zeros((8, LANES), f32)
    for s in range(4):
        standard = (conv_ref[s] - stats_ref[1:2, :]) * inv_std
        scaled = affine_ref[0:1, :] * standard + affine_ref[1:2, :]
        logistic = jax.nn.sigmoid(scaled)
        hidden = scaled * logistic
        hidden_ref[s] = hidden[EDGE : EDGE + frames].astype(bf16)
        grad = back_ref[s] * logistic * (1.0 + scaled * (1.0 - logistic))
        grad_ref[s] = grad
        inner = grad[EDGE : EDGE + frames]
        gain_sum = gain_sum + fold(inner * standard[EDGE : EDGE + frames])
        bias_sum = bias_sum + fold(inner)
    for tap in range(KERNEL):
        begin = HALO - HALF + tap
        acc = jnp.zeros((8, LANES), f32)
        for s in range(4):
            acc = acc + fold(grad_ref[s, EDGE : EDGE + frames, :] * masked_ref[s, begin : begin + frames, :])
        sums_ref[tap : tap + 1, :] = squash(acc)
    sums_ref[KERNEL : KERNEL + 1, :] = squash(gain_sum)
    sums_ref[KERNEL + 1 : KERNEL + 2, :] = squash(bias_sum)
    sums_ref[KERNEL + 2 : KERNEL + 3, :] = jnp.zeros((1, LANES), f32)


def input_kernel(meta_ref, conv_ref, grad_ref, stats_ref, affine_ref, sums_ref, taps_ref, out_ref, back):
    span = conv_ref.shape[1]
    frames = span - 2 * EDGE
    count = jnp.full((1, LANES), meta_ref[5], jnp.int32).astype(f32)
    inv_std = lax.rsqrt(stats_ref[2:3, :] / count + norm_eps)
    gain = affine_ref[0:1, :]
    gain_part = gain * sums_ref[KERNEL : KERNEL + 1, :] / count
    bias_part = gain * sums_ref[KERNEL + 1 : KERNEL + 2, :] / count
    for s in range(4):
        standard = (conv_ref[s] - stats_ref[1:2, :]) * inv_std
        grad = inv_std * (gain * grad_ref[s] - bias_part - standard * gain_part)
        back[s] = jnp.where(valid_in(meta_ref, s, frames, EDGE), grad, 0.0)
        valid = valid_in(meta_ref, s, frames, 0)
        half = frames // 2
        for part in range(2):
            acc = jnp.zeros((half, LANES), f32)
            for tap in range(KERNEL):
                begin = EDGE + HALF - tap + part * half
                acc = acc + taps_ref[tap : tap + 1, :] * back[s, begin : begin + half, :]
            rows = slice(part * half, (part + 1) * half)
            out_ref[s, rows, :] = jnp.where(valid[rows], acc, 0.0).astype(bf16)


def by_lanes(kernel, ins, outs, scratch=(), meta=None):
    def spec(array):
        lead = array.shape[:-1]
        return pl.BlockSpec(lead + (LANES,), lambda i, *_: (0,) * len(lead) + (i,))

    shapes = [jax.ShapeDtypeStruct(shape, dtype) for shape, dtype in outs]
    prefetch = [] if meta is None else [meta]
    return pl.pallas_call(
        kernel,
        out_shape=shapes,
        grid_spec=pltpu.PrefetchScalarGridSpec(
            num_scalar_prefetch=len(prefetch),
            grid=(ins[0].shape[-1] // LANES,),
            in_specs=[spec(x) for x in ins],
            out_specs=[spec(x) for x in shapes],
            scratch_shapes=list(scratch),
        ),
        compiler_params=pltpu.CompilerParams(vmem_limit_bytes=VMEM_LIMIT),
    )(*prefetch, *ins)


def on_device(
    glu_out, lengths, kernel, gain, bias, weight, master, moment_one, moment_two, cotangent
):
    frames, width = glu_out.shape[1:]
    dp = lax.axis_index(DP)
    seq = lax.axis_index(SEQ)
    own = width // 4

    glu_out, cotangent = glu_out[0], cotangent[0]
    below = jnp.concatenate([glu_out[frames - HALO :], cotangent[frames - EDGE :]])
    above = jnp.concatenate([glu_out[:HALO], cotangent[:EDGE]])
    below, above, weight = barrier((below, above, weight))
    low, high = shift(below, SEQ, 1), shift(above, SEQ, -1)
    rows = exchange(weight, "x")
    low, high, rows, lengths, kernel, gain, bias = barrier(
        (low, high, rows, lengths, kernel, gain, bias)
    )
    cot = jnp.concatenate([low[HALO:], cotangent, high[HALO:]], axis=0)
    slab = jnp.concatenate([low[:HALO], glu_out, high[:HALO]], axis=0)
    pick = lambda m: lax.dynamic_slice_in_dim(slab, (dp ^ m) * own, own, axis=1)
    pieces = [pick(0)] + [swap(pick(m), DP, m) for m in (1, 2, 3)]
    total = jnp.sum(lengths)
    count = total.astype(f32)
    places = jnp.arange(4, dtype=jnp.int32)
    limit = jnp.sum(jnp.where(places[None, :] == (dp ^ places)[:, None], lengths, 0), axis=1)
    meta = jnp.concatenate([limit, jnp.stack([seq, total])])

    rows, pieces[1] = barrier((rows, pieces[1]))
    rows = jnp.concatenate(in_order(lax.axis_index("x"), rows), axis=0)
    rows = jnp.stack(in_order(lax.axis_index("zh"), exchange(rows, "zh")), axis=0)
    slabs = jnp.stack(pieces)
    slabs, meta = barrier((slabs, meta))

    def valid_rows(extra):
        positions = seq * frames - extra + jnp.arange(frames + 2 * extra, dtype=jnp.int32)
        return ((positions >= 0) & (positions < limit[:, None]))[:, :, None]

    def mine(table):
        return lax.dynamic_slice_in_dim(table, dp * own, own, axis=table.ndim - 1)

    taps, affine = mine(kernel), mine(jnp.stack([gain, bias]))
    gain_own = affine[0:1]

    span = frames + 2 * EDGE
    masked, conv_out, stats = by_lanes(
        conv_kernel,
        [slabs, taps],
        [((4, frames + 2 * HALO, own), f32), ((4, span, own), f32), ((3, own), f32)],
        meta=meta,
    )
    mean = stats[1:2]
    stats, cot, affine, rows = barrier((stats, cot, affine, rows))

    cot_z = swap(cot, "zl", 1)
    pair = swap(jnp.stack([cot, cot_z]), "core", 1)
    stats = combine(stats, *STAGES[0])
    stats, rows, mean = barrier((stats, rows, mean))
    rows = jnp.stack(in_order(lax.axis_index("y"), exchange(rows, "y")), axis=1).reshape(own, width)
    grad_out = jnp.stack([cot, pair[0], cot_z, pair[1]])
    grad_out = jnp.where(valid_rows(EDGE), grad_out, jnp.zeros((), bf16))
    hidden_grad = lax.dot_general(
        grad_out.reshape(4 * span, width), rows, (((1,), (1,)), ((), ())), preferred_element_type=f32
    ).reshape(4, span, own)

    tap_in, tap_off = by_lanes(
        moment_kernel,
        [masked, conv_out, mean],
        [((KERNEL, own), f32)] * 2,
        [pltpu.VMEM((4, frames, LANES), f32)] * 2,
        meta=meta,
    )
    for axis, mask in STAGES[1:4]:
        stats = combine(stats, axis, mask)
    grad_inner = grad_out[:, EDGE : EDGE + frames].reshape(4 * frames, width)
    stats, hidden_grad, tap_in, tap_off, grad_inner = barrier(
        (stats, hidden_grad, tap_in, tap_off, grad_inner)
    )
    for axis, mask in STAGES[4:]:
        stats = combine(stats, axis, mask)

    hidden, scaled_grad, sums = by_lanes(
        gate_kernel,
        [conv_out, hidden_grad, masked, stats, affine],
        [((4, frames, own), bf16), ((4, span, own), f32), ((KERNEL + 3, own), f32)],
        meta=meta,
    )
    channel_mean = stats[1:2]
    inv_std = lax.rsqrt(stats[2:3] / count + norm_eps)
    tap_off = inv_std * (tap_off + (mean - channel_mean) * tap_in)
    sums = jnp.concatenate([sums, tap_in, tap_off])

    flat = hidden.reshape(4 * frames, own)
    weight_grad = lax.dot_general(
        flat,
        grad_inner,
        (((0,), (0,)), ((), ())),
        preferred_element_type=f32,
    ).reshape(4, 4, own // 16, width)
    product = jnp.dot(flat, rows, preferred_element_type=f32).reshape(4, frames, width)

    weight_grad, sums = scatter_stage(weight_grad, sums, "y", 1)
    other = swap(jnp.stack([product[1], product[3]]).astype(bf16), "core", 1).astype(f32)
    kept, far = product[0] + other[0], product[2] + other[1]
    weight_grad, sums = scatter_stage(weight_grad, sums, "zh", 0)
    sums, far = barrier((sums, far))
    product = kept + swap(far.astype(bf16), "zl", 1).astype(f32)
    weight_grad, sums = scatter_stage(weight_grad.reshape(4, own // 64, width), sums, "x", 0)
    stream_valid = (seq * frames + jnp.arange(frames, dtype=jnp.int32) < limit[0])[:, None]
    module_out = jnp.where(stream_valid, product, 0.0).astype(bf16)

    (flipped,) = by_lanes(
        input_kernel,
        [conv_out, scaled_grad, stats, affine, sums, taps],
        [((4, frames, own), bf16)],
        [pltpu.VMEM((4, span, LANES), f32)],
        meta=meta,
    )
    near = swap(jnp.stack([flipped[1], flipped[3]]), "core", 1)
    near, sums = barrier((near, sums))
    gain_grad, bias_grad = sums[KERNEL : KERNEL + 1], sums[KERNEL + 1 : KERNEL + 2]
    tap_in, tap_off = sums[KERNEL + 3 : 2 * KERNEL + 3], sums[2 * KERNEL + 3 :]
    tap_sums = (inv_std * gain_own) * (
        sums[:KERNEL] - bias_grad / count * tap_in - gain_grad / count * tap_off
    )
    table = jnp.concatenate([tap_sums, sums[KERNEL : KERNEL + 2]], axis=0)
    far = swap(jnp.stack([flipped[2], near[1]]), "zl", 1)
    input_grad = jnp.concatenate(in_order(dp, [flipped[0], near[0], far[0], far[1]]), axis=1)
    table = side_by_side(side_by_side(table, "core"), "zl")

    new_one = beta_one * moment_one + (1.0 - beta_one) * weight_grad
    new_two = beta_two * moment_two + (1.0 - beta_two) * weight_grad * weight_grad
    new_master = master - adam_rate * (new_one / first_fix) / (
        jnp.sqrt(new_two / second_fix) + adam_eps
    )
    return (
        module_out[None],
        input_grad[None],
        table[:KERNEL],
        table[KERNEL],
        table[KERNEL + 1],
        new_master,
        new_one,
        new_two,
    )


def solution(mesh):
    fine = Mesh(mesh.devices.reshape(2, 2, 4, 4, 4), DP + SEQ)
    whole, split, tall = P(), P(DP, SEQ, None), P(DP + SEQ, None)
    return jax.shard_map(
        on_device,
        mesh=fine,
        in_specs=(split, whole, whole, whole, whole, tall, tall, tall, tall, split),
        out_specs=(split, split, whole, whole, whole, tall, tall, tall),
        check_vma=False,
    )
```
